512 devices in a mesh: rows: 64 (over z, x), inner: 8 (over y, core).
Axes of the slice: x: 4, y: 4, z: 16, core: 2. Of those that a mesh axis runs over, the one named last changes fastest.
Arguments:
- blocks: bfloat16 [64, 16, 256, 256], P('rows'), may hold values from -0.375 to 0.375
- columns: int32 [64, 16], replicated, may hold values from -1 to 63, as said below
Outputs:
- purified: float32 [64, 16, 256, 256], P('rows', None, 'inner')
The draws below stay inside these ranges and needn't reach their ends.
Inputs may be any that keep to these rules, and one draw needn't show every extreme that they name: Each entry of row i that is not -1 is (i + d) mod 64 for an offset d with -16 <= 2 * d < 16; the entries of a row are distinct and stand before its -1 entries; every row lists its diagonal block; some row lists 16 columns.
All inputs are finite; a program needn't handle non-finite values.
Results may differ from the reference program's by a relative error of at most 0.0055.
Values may be sent and summed in bfloat16 or wider, within the bound.
No kernel may reach another device: no remote copies, remote signals or barrier semaphores. Data moves between devices by JAX's collectives and lax.ppermute only.
A program may use at most 128 MiB of HBM per device.

```python
import jax
import jax.numpy as jnp
from jax import lax

BS = 256
BAND = 16
NB = 64
N_INNER = 8


def draw_columns(key, part):
    half_band = BAND // 2
    first_key, second_key, third_key = jax.random.split(jax.random.fold_in(key, 11), 3)
    density = jax.random.randint(first_key, (NB, 1), 24, 96)
    rolls = jax.random.randint(second_key, (NB, BAND), 0, 64)
    slot_ids = jnp.arange(BAND, dtype=jnp.int32)
    distance = 3 * jnp.abs(slot_ids - half_band)
    live_slots = rolls < density - distance[None, :]
    full_row = jax.random.randint(third_key, (), 0, NB)
    row_ids = jnp.arange(NB, dtype=jnp.int32)
    live_slots = live_slots | (slot_ids[None, :] == half_band) | (row_ids[:, None] == full_row)
    sort_keys = jnp.where(live_slots, slot_ids[None, :], slot_ids[None, :] + BAND)
    order = jnp.argsort(sort_keys, axis=1, stable=True).astype(jnp.int32)
    live_sorted = jnp.take_along_axis(live_slots, order, axis=1)
    block_cols = (row_ids[:, None] + order - half_band) % NB
    return jnp.where(live_sorted, block_cols, -1).astype(jnp.int32)


def block_levels(key, dims, shards, least, largest):
    factor_of, own = 1.0, jax.random.fold_in(key, 6)
    for axis_at, shards_of in shards:
        heights = jnp.exp(jax.random.uniform(jax.random.fold_in(own, axis_at), (shards_of,), jnp.float32, least / len(shards), largest / len(shards)))
        factor_of = factor_of * jnp.repeat(heights, dims[axis_at] // shards_of).reshape([-1 if axis == axis_at else 1 for axis in range(len(dims))])
    return factor_of


def gaussian(stream_key, shape, width, reach, cuts=(), held_as=jnp.bfloat16):
    entries = width * jax.random.normal(stream_key, shape, jnp.float32)
    if cuts:
        entries = entries * block_levels(stream_key, shape, cuts, -0.22, 0.18)
    return jnp.clip(entries, -reach, reach).astype(held_as)


def setup_inputs(seed: int = 0) -> dict:
    arg_keys = jax.random.split(jax.random.key(seed), 3)
    blocks = gaussian(arg_keys[0], (NB, BAND, BS, BS), BS ** -0.5, 0.375, ((0, 64),))
    columns = draw_columns(jax.random.fold_in(arg_keys[2], 71), 0)
    return dict(blocks=blocks, columns=columns)


def live_table(columns):
    nrows, band_width = columns.shape
    half_band = band_width // 2
    row_ids = jnp.arange(nrows, dtype=jnp.int32)
    target = (row_ids[:, None] + jnp.arange(band_width, dtype=jnp.int32)[None, :] - half_band) % nrows
    return jnp.any(columns[:, None, :] == target[:, :, None], axis=2)


def slot_shift(piece, delta):
    band_width = piece.shape[1]
    if delta >= 0:
        return jnp.concatenate([piece[:, delta:], jnp.zeros_like(piece[:, :delta])], axis=1)
    return jnp.concatenate([jnp.zeros_like(piece[:, :(-delta)]), piece[:, :band_width + delta]], axis=1)


def band_product(left_all, right_all):
    nrows, band_width, block_size, _ = left_all.shape
    half_band = band_width // 2
    slab_width = block_size // N_INNER

    def one_row(row_index):
        row_ids = (row_index + jnp.arange(band_width, dtype=jnp.int32) - half_band) % nrows
        right_rows = right_all[row_ids]
        left_rows = left_all[row_index]
        totals = jnp.zeros((N_INNER, band_width, block_size, block_size), jnp.float32)
        for offset in range(band_width):
            shifted = slot_shift(right_rows[offset][None], half_band - offset)[0]
            left_slab = left_rows[offset].astype(jnp.float32).reshape(block_size, N_INNER, slab_width)
            right_slab = shifted.astype(jnp.float32).reshape(band_width, N_INNER, slab_width, block_size)
            totals = totals + jnp.einsum("mcq,scqn->csmn", left_slab, right_slab)
        rounded = lax.optimization_barrier(totals.astype(jnp.bfloat16))
        return jnp.sum(rounded.astype(jnp.float32), axis=0)

    return lax.map(one_row, jnp.arange(nrows, dtype=jnp.int32))


def reference(blocks, columns):
    live_slots = live_table(columns)[:, :, None, None]
    masked = jnp.where(live_slots, blocks, jnp.zeros_like(blocks))
    square = jnp.where(live_slots, band_product(masked, masked), jnp.float32(0.0)).astype(jnp.bfloat16)
    cubed = jnp.where(live_slots, band_product(masked, square), jnp.float32(0.0))
    return 3.0 * square.astype(jnp.float32) - 2.0 * cubed
```

```python
import functools

import jax
import jax.numpy as jnp
from jax import lax
from jax.experimental import pallas as pl
from jax.experimental.pallas import tpu as pltpu
from jax.sharding import Mesh
from jax.sharding import PartitionSpec as P

BS = 256
BAND = 16
NB = 64
NZ, NX, NY, NC = 16, 4, 4, 2
SLAB = 32
ROWS = BAND * SLAB
BF = jnp.bfloat16
F32 = jnp.float32


def shift(value, axis, steps):
    count = lax.axis_size(axis)
    return lax.ppermute(value, axis, [(s, (s + steps) % count) for s in range(count)])


def band_kernel(last, place, own, up1, up2, down1, down2, left0, left_a, left_b, out, padded):
    x, c = place[0], place[1]
    edge = 8 * SLAB
    for dz in range(5):
        padded[dz, :edge, :] = jnp.zeros((edge, BS), BF)
        padded[dz, 3 * edge :, :] = jnp.zeros((edge, BS), BF)
    padded[2, edge : edge + ROWS, :] = own[...]
    padded[3, edge : edge + 15 * SLAB, :] = up1[...]
    padded[4, edge : edge + 11 * SLAB, :] = up2[...]
    padded[1, edge + SLAB : edge + ROWS, :] = down1[...]
    padded[0, edge + 5 * SLAB : edge + ROWS, :] = down2[...]
    contract = (((1,), (1,)), ((), ()))
    for e in range(4):
        wrapped = jnp.where(x < e, 1, 0)
        total = None
        for q in range(4):
            if e == 0:
                block = left0[q]
                turn = q
            else:
                block = left_a[e - 1, q] if q < 2 else left_b[e - 1, q - 2]
                turn = 2 * (c if q < 2 else 1 - c) + q % 2
            start = (16 - e - 4 * turn) * SLAB
            if e:
                start = pl.multiple_of(start, SLAB)
            rows = padded[turn + wrapped, pl.ds(start, ROWS), :]
            term = lax.dot_general(rows, block, contract, preferred_element_type=F32)
            total = term if total is None else total + term
        if last and e == 0:
            total = total - 1.5 * own[...].astype(F32)
        target = lax.rem(x - e + 4, 4)
        if not last:
            out[target] = total.astype(BF)
            continue
        for h in range(2):
            lane = lax.broadcasted_iota(jnp.int32, (128, 128), 1) // SLAB
            for g in range(4):
                packed = None
                for sh in range(4):
                    piece = total[sh * 128 : sh * 128 + 128, h * 128 : h * 128 + 128]
                    if sh != g:
                        piece = pltpu.roll(piece, ((sh - g) % 4) * SLAB, 1)
                    packed = piece if packed is None else jnp.where(lane == sh, piece, packed)
                out[target * 8 + h * 4 + g] = packed.astype(BF)


def band_terms(place, window, left, last):
    shape = (32, 128, 128) if last else (4, ROWS, BS)
    vmem = pl.BlockSpec(memory_space=pltpu.VMEM)
    return pl.pallas_call(
        functools.partial(band_kernel, last),
        out_shape=jax.ShapeDtypeStruct(shape, BF),
        in_specs=[pl.BlockSpec(memory_space=pltpu.SMEM)] + [vmem] * 8,
        out_specs=vmem,
        scratch_shapes=[pltpu.VMEM((5, 4 * 8 * SLAB, BS), BF)],
        compiler_params=pltpu.CompilerParams(vmem_limit_bytes=40 * 2**20),
        cost_estimate=pl.CostEstimate(
            flops=2 * 16 * ROWS * BS * BS, bytes_accessed=6 * 2**20, transcendentals=0
        ),
        name="cube_terms" if last else "square_terms",
    )(place, *window, *left)


def finish_kernel(parts, out):
    total = parts[0].astype(F32)
    for x in range(1, 4):
        total = total + parts[x].astype(F32)
    total = -2.0 * total
    for lo in range(4):
        tile = total[:, lo * SLAB : lo * SLAB + SLAB, :].reshape(BS, 128)
        flat = tile.T
        for hi in range(4):
            out[hi * 4 + lo] = flat[hi * SLAB : hi * SLAB + SLAB, :]


def finish(parts):
    vmem = pl.BlockSpec(memory_space=pltpu.VMEM)
    return pl.pallas_call(
        finish_kernel,
        out_shape=jax.ShapeDtypeStruct((BAND, SLAB, BS), F32),
        in_specs=[vmem],
        out_specs=vmem,
        compiler_params=pltpu.CompilerParams(vmem_limit_bytes=40 * 2**20),
        name="finish",
    )(parts)


def band_window(own):
    up1 = shift(own[: 15 * SLAB], "z", -1)
    down1 = shift(own[SLAB:], "z", 1)
    up2 = shift(own[: 11 * SLAB], "z", -2)
    down2 = shift(own[5 * SLAB :], "z", 2)
    return own, up1, up2, down1, down2


def per_device(blocks, columns):
    z, x, y, c = (lax.axis_index(name) for name in ("z", "x", "y", "core"))
    row = z * NX + x
    listed = lax.dynamic_slice_in_dim(columns, row, 1, 0)
    target = (row + jnp.arange(BAND, dtype=jnp.int32) - BAND // 2) % NB
    live = jnp.any(listed == target[:, None], axis=1)[:, None, None]
    place = jnp.stack([x, c]).astype(jnp.int32)

    masked = jnp.where(live, blocks[0], jnp.zeros_like(blocks[0]))
    slab = y * NC + c
    pick = (jnp.arange(BS)[None, :] == slab * SLAB + jnp.arange(SLAB)[:, None]).astype(BF)
    own = jnp.einsum("pn,skn->spk", pick, masked, preferred_element_type=F32)
    own = own.astype(BF).reshape(ROWS, BS)

    quarters = masked.reshape(4, 4, BS, BS)
    half = lax.dynamic_slice_in_dim(quarters, 2 * c, 2, 0)
    left_a = jnp.stack([shift(half[:, e], "x", e) for e in (1, 2, 3)])
    left_b = shift(left_a, "core", 1)
    left = (quarters[:, 0], left_a, left_b)

    terms = band_terms(place, band_window(own), left, False)
    parts = lax.all_to_all(terms, "x", 0, 0, tiled=True)
    square = jnp.sum(parts.astype(F32), axis=0).reshape(BAND, SLAB, BS)
    square = jnp.where(live, square, 0.0).astype(BF).reshape(ROWS, BS)

    terms = band_terms(place, band_window(square), left, True)
    parts = lax.all_to_all(terms, ("x", "y", "core"), 0, 0, tiled=True)
    result = finish(parts.reshape(4, 8, 128, 128))
    return jnp.where(live, result, 0.0)[None]


def solution(mesh):
    grid = Mesh(mesh.devices.reshape(NZ, NX, NY, NC), ("z", "x", "y", "core"))
    return jax.shard_map(
        per_device,
        mesh=grid,
        in_specs=(P(("z", "x"), None, None, None), P()),
        out_specs=P(("z", "x"), None, ("y", "core"), None),
        check_vma=False,
    )
```

```python
import functools

import jax
import jax.numpy as jnp
from jax import lax
from jax.experimental import pallas as pl
from jax.experimental.pallas import tpu as pltpu
from jax.sharding import Mesh
from jax.sharding import PartitionSpec as P

BS = 256
BAND = 16
NB = 64
NZ, NX, NY, NC = 16, 4, 4, 2
SLAB = 32
ROWS = BAND * SLAB
BF = jnp.bfloat16
F32 = jnp.float32


def shift(value, axis, steps):
    count = lax.axis_size(axis)
    return lax.ppermute(value, axis, [(s, (s + steps) % count) for s in range(count)])


def band_kernel(last, place, own, up1, up2, down1, down2, left_a, left_b, out, padded):
    x, c = place[0], place[1]
    edge = 8 * SLAB
    for dz in range(5):
        padded[dz, :edge, :] = jnp.zeros((edge, BS), BF)
        padded[dz, 3 * edge :, :] = jnp.zeros((edge, BS), BF)
    padded[2, edge : edge + ROWS, :] = own[...]
    padded[3, edge : edge + 15 * SLAB, :] = up1[...]
    padded[4, edge : edge + 11 * SLAB, :] = up2[...]
    padded[1, edge + SLAB : edge + ROWS, :] = down1[...]
    padded[0, edge + 5 * SLAB : edge + ROWS, :] = down2[...]
    contract = (((1,), (1,)), ((), ()))
    for e in range(4):
        wrapped = jnp.where(x < e, 1, 0)
        target = lax.rem(x - e + 4, 4)
        total = None
        for q in range(4):
            block = left_a[target, q] if q < 2 else left_b[target, q - 2]
            turn = 2 * (c if q < 2 else 1 - c) + q % 2
            start = pl.multiple_of((16 - e - 4 * turn) * SLAB, SLAB)
            rows = padded[turn + wrapped, pl.ds(start, ROWS), :]
            term = lax.dot_general(rows, block, contract, preferred_element_type=F32)
            total = term if total is None else total + term
        if last and e == 0:
            total = total - 1.5 * own[...].astype(F32)
        if not last:
            out[target] = total.astype(BF)
            continue
        for h in range(2):
            lane = lax.broadcasted_iota(jnp.int32, (128, 128), 1) // SLAB
            for g in range(4):
                packed = None
                for sh in range(4):
                    piece = total[sh * 128 : sh * 128 + 128, h * 128 : h * 128 + 128]
                    if sh != g:
                        piece = pltpu.roll(piece, ((sh - g) % 4) * SLAB, 1)
                    packed = piece if packed is None else jnp.where(lane == sh, piece, packed)
                out[target * 8 + h * 4 + g] = packed.astype(BF)


def band_terms(place, window, left, last):
    shape = (32, 128, 128) if last else (4, ROWS, BS)
    vmem = pl.BlockSpec(memory_space=pltpu.VMEM)
    return pl.pallas_call(
        functools.partial(band_kernel, last),
        out_shape=jax.ShapeDtypeStruct(shape, BF),
        in_specs=[pl.BlockSpec(memory_space=pltpu.SMEM)] + [vmem] * 7,
        out_specs=vmem,
        scratch_shapes=[pltpu.VMEM((5, 4 * 8 * SLAB, BS), BF)],
        compiler_params=pltpu.CompilerParams(vmem_limit_bytes=40 * 2**20),
        cost_estimate=pl.CostEstimate(
            flops=2 * 16 * ROWS * BS * BS, bytes_accessed=6 * 2**20, transcendentals=0
        ),
        name="cube_terms" if last else "square_terms",
    )(place, *window, *left)


def finish_kernel(live, parts, out):
    total = parts[0].astype(F32)
    for x in range(1, 4):
        total = total + parts[x].astype(F32)
    total = -2.0 * total
    for lo in range(4):
        tile = total[:, lo * SLAB : lo * SLAB + SLAB, :].reshape(BS, 128)
        flat = tile.T
        for hi in range(4):
            slot = hi * 4 + lo
            piece = flat[hi * SLAB : hi * SLAB + SLAB, :]
            out[slot] = jnp.where(live[slot] > 0, piece, 0.0)


def finish(live, parts):
    vmem = pl.BlockSpec(memory_space=pltpu.VMEM)
    return pl.pallas_call(
        finish_kernel,
        out_shape=jax.ShapeDtypeStruct((BAND, SLAB, BS), F32),
        in_specs=[pl.BlockSpec(memory_space=pltpu.SMEM), vmem],
        out_specs=vmem,
        compiler_params=pltpu.CompilerParams(vmem_limit_bytes=40 * 2**20),
        name="finish",
    )(live, parts)


def prepare_kernel(place, live, blocks, own, sent):
    step = pl.program_id(0)
    x, c, slab = place[0], place[1], place[2]
    base = pl.multiple_of((slab // 4) * 128, 128)
    column = lax.broadcasted_iota(jnp.int32, (SLAB, 128), 1)
    pick = column == lax.rem(slab, 4) * SLAB + lax.broadcasted_iota(jnp.int32, (SLAB, 128), 0)
    for e in range(4):
        chosen = jnp.where(pick & (live[4 * step + e] > 0), 1.0, 0.0).astype(BF)
        part = lax.dot_general(
            chosen,
            blocks[e, :, pl.ds(base, 128)],
            (((1,), (1,)), ((), ())),
            preferred_element_type=F32,
        )
        own[e * SLAB : e * SLAB + SLAB, :] = part.astype(BF)

    @pl.when(step // 2 == c)
    def _():
        for e in range(4):
            kept = jnp.where(live[4 * step + e] > 0, blocks[e], jnp.zeros((BS, BS), BF))
            sent[lax.rem(x + e, 4), lax.rem(step, 2)] = kept


def prepare(place, live, blocks):
    smem = pl.BlockSpec(memory_space=pltpu.SMEM)
    return pl.pallas_call(
        prepare_kernel,
        grid=(4,),
        out_shape=(
            jax.ShapeDtypeStruct((ROWS, BS), BF),
            jax.ShapeDtypeStruct((4, 2, BS, BS), BF),
        ),
        in_specs=[smem, smem, pl.BlockSpec((4, BS, BS), lambda q: (q, 0, 0))],
        out_specs=(
            pl.BlockSpec((4 * SLAB, BS), lambda q: (q, 0)),
            pl.BlockSpec((4, 2, BS, BS), lambda q: (0, 0, 0, 0)),
        ),
        compiler_params=pltpu.CompilerParams(vmem_limit_bytes=40 * 2**20),
        name="prepare",
    )(place, live, blocks)


def band_window(own):
    up1 = shift(own[: 15 * SLAB], "z", -1)
    down1 = shift(own[SLAB:], "z", 1)
    up2 = shift(own[: 11 * SLAB], "z", -2)
    down2 = shift(own[5 * SLAB :], "z", 2)
    return own, up1, up2, down1, down2


def per_device(blocks, columns):
    z, x, y, c = (lax.axis_index(name) for name in ("z", "x", "y", "core"))
    row = z * NX + x
    listed = lax.dynamic_slice_in_dim(columns, row, 1, 0)
    target = (row + jnp.arange(BAND, dtype=jnp.int32) - BAND // 2) % NB
    live = jnp.any(listed == target[:, None], axis=1)
    live_flags = live.astype(jnp.int32)
    live = live[:, None, None]
    place = jnp.stack([x, c, y * NC + c]).astype(jnp.int32)

    own, sent = prepare(place, live_flags, blocks[0])
    left_a = lax.all_to_all(sent, "x", 0, 0, tiled=True)
    window = band_window(own)
    first = tuple(window[k] for k in (1, 2, 3, 4))
    left_a, first = lax.optimization_barrier((left_a, first))
    window = tuple(dict(zip((1, 2, 3, 4), first)).get(k, part) for k, part in enumerate(window))
    left_b = shift(left_a, "core", 1)
    left = (left_a, left_b)

    terms = band_terms(place, window, left, False)
    parts = lax.all_to_all(terms, "x", 0, 0, tiled=True)
    square = jnp.sum(parts.astype(F32), axis=0).reshape(BAND, SLAB, BS)
    square = jnp.where(live, square, 0.0).astype(BF).reshape(ROWS, BS)

    terms = band_terms(place, band_window(square), left, True)
    parts = lax.all_to_all(terms, ("x", "y", "core"), 0, 0, tiled=True)
    return finish(live_flags, parts.reshape(4, 8, 128, 128))[None]


def solution(mesh):
    grid = Mesh(mesh.devices.reshape(NZ, NX, NY, NC), ("z", "x", "y", "core"))
    return jax.shard_map(
        per_device,
        mesh=grid,
        in_specs=(P(("z", "x"), None, None, None), P()),
        out_specs=P(("z", "x"), None, ("y", "core"), None),
        check_vma=False,
    )
```

```python
import functools

import jax
import jax.numpy as jnp
from jax import lax
from jax.experimental import pallas as pl
from jax.experimental.pallas import tpu as pltpu
from jax.sharding import Mesh
from jax.sharding import PartitionSpec as P

BS = 256
BAND = 16
NB = 64
NZ, NX, NY, NC = 16, 4, 4, 2
SLAB = 32
ROWS = BAND * SLAB
BF = jnp.bfloat16
F32 = jnp.float32
MINE = NX + 2


READ = ((0, 15), (0, 11), (1, 16), (5, 16))
HOPS = (-1, -2, 1, 2)
OUTGOING = tuple(jax.ShapeDtypeStruct(((hi - lo) * SLAB, BS), BF) for lo, hi in READ)


def shift(value, axis, steps):
    count = lax.axis_size(axis)
    return lax.ppermute(value, axis, [(s, (s + steps) % count) for s in range(count)])


def band_kernel(last, flags, own, up1, up2, down1, down2, left, out, padded):
    x = lax.axis_index("x")
    edge = 8 * SLAB
    for dz in range(5):
        padded[dz, :edge, :] = jnp.zeros((edge, BS), BF)
        padded[dz, 3 * edge :, :] = jnp.zeros((edge, BS), BF)
    padded[5] = jnp.zeros((4 * edge, BS), BF)
    for dz, part, (lo, hi) in zip(
        (2, 3, 4, 1, 0), (own, up1, up2, down1, down2), ((0, BAND), *READ)
    ):
        if last:
            padded[dz, edge + lo * SLAB : edge + hi * SLAB, :] = part[...]
            continue
        for slot in range(lo, hi):
            piece = part[(slot - lo) * SLAB : (slot - lo + 1) * SLAB, :]
            piece = jnp.where(flags[4 + dz, slot] > 0, piece, jnp.zeros((SLAB, BS), BF))
            padded[dz, edge + slot * SLAB : edge + (slot + 1) * SLAB, :] = piece
    contract = (((1,), (1,)), ((), ()))
    for e in range(4):
        wrapped = jnp.where(x < e, 1, 0)
        target = lax.rem(x - e + 4, 4)
        total = None
        for q in range(4):
            start = (16 - e - 4 * q) * SLAB
            plane = jnp.where(flags[target, 4 * q + e] > 0, q + wrapped, 5)
            rows = padded[plane, start : start + ROWS, :]
            term = lax.dot_general(rows, left[target, q], contract, preferred_element_type=F32)
            total = term if total is None else total + term
        if last and e == 0:
            total = total - 1.5 * own[...].astype(F32)
        if not last:
            out[target] = total.astype(BF)
            continue
        for h in range(2):
            lane = lax.broadcasted_iota(jnp.int32, (128, 128), 1) // SLAB
            for g in range(4):
                packed = None
                for sh in range(4):
                    piece = total[sh * 128 : sh * 128 + 128, h * 128 : h * 128 + 128]
                    if sh != g:
                        piece = pltpu.roll(piece, ((sh - g) % 4) * SLAB, 1)
                    packed = piece if packed is None else jnp.where(lane == sh, piece, packed)
                out[target * 8 + h * 4 + g] = packed.astype(BF)


def band_terms(flags, window, left, last):
    shape = (32, 128, 128) if last else (4, ROWS, BS)
    vmem = pl.BlockSpec(memory_space=pltpu.VMEM)
    return pl.pallas_call(
        functools.partial(band_kernel, last),
        out_shape=jax.ShapeDtypeStruct(shape, BF),
        in_specs=[pl.BlockSpec(memory_space=pltpu.SMEM)] + [vmem] * 6,
        out_specs=vmem,
        scratch_shapes=[pltpu.VMEM((6, 4 * 8 * SLAB, BS), BF)],
        compiler_params=pltpu.CompilerParams(vmem_limit_bytes=40 * 2**20),
        cost_estimate=pl.CostEstimate(
            flops=2 * 16 * ROWS * BS * BS, bytes_accessed=6 * 2**20, transcendentals=0
        ),
        name="cube_terms" if last else "square_terms",
    )(flags, *window, left)


def finish_kernel(flags, parts, out):
    total = parts[0].astype(F32)
    for x in range(1, 4):
        total = total + parts[x].astype(F32)
    total = -2.0 * total
    for lo in range(4):
        tile = total[:, lo * SLAB : lo * SLAB + SLAB, :].reshape(BS, 128)
        flat = tile.T
        for hi in range(4):
            slot = hi * 4 + lo
            piece = flat[hi * SLAB : hi * SLAB + SLAB, :]
            out[slot] = jnp.where(flags[MINE, slot] > 0, piece, 0.0)


def finish(flags, parts):
    vmem = pl.BlockSpec(memory_space=pltpu.VMEM)
    return pl.pallas_call(
        finish_kernel,
        out_shape=jax.ShapeDtypeStruct((BAND, SLAB, BS), F32),
        in_specs=[pl.BlockSpec(memory_space=pltpu.SMEM), vmem],
        out_specs=vmem,
        compiler_params=pltpu.CompilerParams(vmem_limit_bytes=40 * 2**20),
        name="finish",
    )(flags, parts)


def band_window(own, outgoing):
    return (own, *(shift(part, "z", hop) for part, hop in zip(outgoing, HOPS)))


def store_slots(value, first, own, outgoing):
    count = value.shape[0] // SLAB
    own[first * SLAB : (first + count) * SLAB, :] = value
    for part, (lo, hi) in zip(outgoing, READ):
        begin, end = max(lo, first), min(hi, first + count)
        if begin < end:
            part[(begin - lo) * SLAB : (end - lo) * SLAB, :] = value[
                (begin - first) * SLAB : (end - first) * SLAB, :
            ]


def prepare_kernel(blocks, own, o1, o2, o3, o4, sent, held, move_sems, load_sems):
    x = lax.axis_index("x")
    slab = lax.axis_index("y") * NC + lax.axis_index("core")
    base = pl.multiple_of((slab // 4) * 128, 128)
    loads = [
        pltpu.make_async_copy(blocks.at[pl.ds(4 * q, 4)], held.at[q], load_sems.at[q])
        for q in range(4)
    ]
    for copy in loads:
        copy.start()
    moves = [
        pltpu.make_async_copy(
            held.at[q, e], sent.at[lax.rem(x + e, 4), q], move_sems.at[4 * q + e]
        )
        for q in range(4)
        for e in range(4)
    ]
    line = lax.broadcasted_iota(jnp.int32, (128, 128), 0) - lax.rem(slab, 4) * SLAB
    column = lax.broadcasted_iota(jnp.int32, (128, 128), 1)
    inside = (line >= 0) & (line < SLAB)
    picks = [
        jnp.where(inside & (column == line + e * SLAB), 1.0, 0.0).astype(BF) for e in range(4)
    ]
    for q in range(4):
        loads[q].wait()
        for e in range(4):
            moves[4 * q + e].start()
        total = None
        for e in range(4):
            part = jnp.dot(
                held[q, e, :, pl.ds(base, 128)], picks[e], preferred_element_type=F32
            )
            total = part if total is None else total + part
        store_slots(total.T.astype(BF), 4 * q, own, (o1, o2, o3, o4))
    for copy in moves:
        copy.wait()


def prepare(blocks):
    vmem = pl.BlockSpec(memory_space=pltpu.VMEM)
    anywhere = pl.BlockSpec(memory_space=pl.ANY)
    return pl.pallas_call(
        prepare_kernel,
        out_shape=(
            jax.ShapeDtypeStruct((ROWS, BS), BF),
            *OUTGOING,
            jax.ShapeDtypeStruct((4, 4, BS, BS), BF),
        ),
        in_specs=[anywhere],
        out_specs=(*(vmem,) * 5, anywhere),
        scratch_shapes=[
            pltpu.VMEM((4, 4, BS, BS), BF),
            pltpu.SemaphoreType.DMA((16,)),
            pltpu.SemaphoreType.DMA((4,)),
        ],
        compiler_params=pltpu.CompilerParams(vmem_limit_bytes=56 * 2**20),
        name="prepare",
    )(blocks)


def gather_kernel(flags, parts, own, o1, o2, o3, o4):
    for slot in range(BAND):
        piece = parts[0, slot * SLAB : slot * SLAB + SLAB, :].astype(F32)
        for x in range(1, 4):
            piece = piece + parts[x, slot * SLAB : slot * SLAB + SLAB, :].astype(F32)
        piece = jnp.where(flags[MINE, slot] > 0, piece, 0.0).astype(BF)
        store_slots(piece, slot, own, (o1, o2, o3, o4))


def gather_square(flags, parts):
    vmem = pl.BlockSpec(memory_space=pltpu.VMEM)
    return pl.pallas_call(
        gather_kernel,
        out_shape=(jax.ShapeDtypeStruct((ROWS, BS), BF), *OUTGOING),
        in_specs=[pl.BlockSpec(memory_space=pltpu.SMEM), vmem],
        out_specs=(vmem,) * 5,
        compiler_params=pltpu.CompilerParams(vmem_limit_bytes=40 * 2**20),
        name="gather_square",
    )(flags, parts)


def per_device(blocks, columns):
    own, *outgoing, sent = prepare(blocks[0])
    left = lax.all_to_all(sent, "x", 0, 0, tiled=True)
    own, *around = band_window(own, outgoing)
    left, around = lax.optimization_barrier((left, around))

    z, x = lax.axis_index("z"), lax.axis_index("x")
    rows = jnp.concatenate(
        [NX * z + jnp.arange(NX), NX * (z + jnp.arange(-2, 3)) + x]
    ).astype(jnp.int32) % NB
    listed = columns[rows]
    target = (rows[:, None] + jnp.arange(BAND, dtype=jnp.int32) - BAND // 2) % NB
    flags = jnp.any(listed[:, None, :] == target[:, :, None], axis=2).astype(jnp.int32)

    terms = band_terms(flags, (own, *around), left, False)
    parts = lax.all_to_all(terms, "x", 0, 0, tiled=True)
    own, *outgoing = gather_square(flags, parts)
    terms = band_terms(flags, band_window(own, outgoing), left, True)
    parts = lax.all_to_all(terms, ("x", "y", "core"), 0, 0, tiled=True)
    return finish(flags, parts.reshape(4, 8, 128, 128))[None]


def solution(mesh):
    grid = Mesh(mesh.devices.reshape(NZ, NX, NY, NC), ("z", "x", "y", "core"))
    return jax.shard_map(
        per_device,
        mesh=grid,
        in_specs=(P(("z", "x"), None, None, None), P()),
        out_specs=P(("z", "x"), None, ("y", "core"), None),
        check_vma=False,
    )
```

```python
import functools

import jax
import jax.numpy as jnp
from jax import lax
from jax.experimental import pallas as pl
from jax.experimental.pallas import tpu as pltpu
from jax.sharding import Mesh
from jax.sharding import PartitionSpec as P

BS = 256
BAND = 16
NB = 64
NZ, NX, NY, NC = 16, 4, 4, 2
SLAB = 32
ROWS = BAND * SLAB
BF = jnp.bfloat16
F32 = jnp.float32
MINE = NX + 2


NEAR, FAR = 15, 11
OUTGOING = (jax.ShapeDtypeStruct((NEAR * SLAB, BS), BF),) * 2


def shift(value, axis, steps):
    count = lax.axis_size(axis)
    return lax.ppermute(value, axis, [(s, (s + steps) % count) for s in range(count)])


def band_kernel(last, flags, own, near_a, near_b, far_a, far_b, left, out, padded):
    x = lax.axis_index("x")
    even = 1 - lax.rem(lax.axis_index("z"), 2)
    odd = 1 - even
    edge = 8 * SLAB
    for dz in range(5):
        padded[dz, :edge, :] = jnp.zeros((edge, BS), BF)
        padded[dz, 3 * edge :, :] = jnp.zeros((edge, BS), BF)
    padded[5] = jnp.zeros((4 * edge, BS), BF)
    for part, dz, lo, count in (
        (own, 2, 0, BAND),
        (near_a, 1 + 2 * even, odd, NEAR),
        (near_b, 1 + 2 * odd, even, NEAR),
        (far_a, 4 * even, 5 * odd, FAR),
        (far_b, 4 * odd, 5 * even, FAR),
    ):
        if last:
            begin = pl.multiple_of(edge + lo * SLAB, SLAB)
            padded[dz, pl.ds(begin, count * SLAB), :] = part[...]
            continue
        for at in range(count):
            piece = part[at * SLAB : (at + 1) * SLAB, :]
            piece = jnp.where(flags[4 + dz, lo + at] > 0, piece, jnp.zeros((SLAB, BS), BF))
            begin = pl.multiple_of(edge + (lo + at) * SLAB, SLAB)
            padded[dz, pl.ds(begin, SLAB), :] = piece
    contract = (((1,), (1,)), ((), ()))
    for e in range(4):
        wrapped = jnp.where(x < e, 1, 0)
        target = lax.rem(x - e + 4, 4)
        total = None
        for q in range(4):
            start = (16 - e - 4 * q) * SLAB
            plane = jnp.where(flags[target, 4 * q + e] > 0, q + wrapped, 5)
            rows = padded[plane, start : start + ROWS, :]
            term = lax.dot_general(rows, left[target, q], contract, preferred_element_type=F32)
            total = term if total is None else total + term
        if last and e == 0:
            total = total - 1.5 * own[...].astype(F32)
        if not last:
            out[target] = total.astype(BF)
            continue
        for h in range(2):
            lane = lax.broadcasted_iota(jnp.int32, (128, 128), 1) // SLAB
            for g in range(4):
                packed = None
                for sh in range(4):
                    piece = total[sh * 128 : sh * 128 + 128, h * 128 : h * 128 + 128]
                    if sh != g:
                        piece = pltpu.roll(piece, ((sh - g) % 4) * SLAB, 1)
                    packed = piece if packed is None else jnp.where(lane == sh, piece, packed)
                out[target * 8 + h * 4 + g] = packed.astype(BF)


def band_terms(flags, window, left, last):
    shape = (32, 128, 128) if last else (4, ROWS, BS)
    vmem = pl.BlockSpec(memory_space=pltpu.VMEM)
    return pl.pallas_call(
        functools.partial(band_kernel, last),
        out_shape=jax.ShapeDtypeStruct(shape, BF),
        in_specs=[pl.BlockSpec(memory_space=pltpu.SMEM)] + [vmem] * 6,
        out_specs=vmem,
        scratch_shapes=[pltpu.VMEM((6, 4 * 8 * SLAB, BS), BF)],
        compiler_params=pltpu.CompilerParams(vmem_limit_bytes=40 * 2**20),
        cost_estimate=pl.CostEstimate(
            flops=2 * 16 * ROWS * BS * BS, bytes_accessed=6 * 2**20, transcendentals=0
        ),
        name="cube_terms" if last else "square_terms",
    )(flags, *window, left)


def finish_kernel(flags, parts, out):
    total = parts[0].astype(F32)
    for x in range(1, 4):
        total = total + parts[x].astype(F32)
    total = -2.0 * total
    for lo in range(4):
        tile = total[:, lo * SLAB : lo * SLAB + SLAB, :].reshape(BS, 128)
        flat = tile.T
        for hi in range(4):
            slot = hi * 4 + lo
            piece = flat[hi * SLAB : hi * SLAB + SLAB, :]
            out[slot] = jnp.where(flags[MINE, slot] > 0, piece, 0.0)


def finish(flags, parts):
    vmem = pl.BlockSpec(memory_space=pltpu.VMEM)
    return pl.pallas_call(
        finish_kernel,
        out_shape=jax.ShapeDtypeStruct((BAND, SLAB, BS), F32),
        in_specs=[pl.BlockSpec(memory_space=pltpu.SMEM), vmem],
        out_specs=vmem,
        compiler_params=pltpu.CompilerParams(vmem_limit_bytes=40 * 2**20),
        name="finish",
    )(flags, parts)


def to_partner(value, kind):
    return lax.ppermute(value, "z", [(z, (((z + kind) ^ 1) - kind) % NZ) for z in range(NZ)])


def band_window(near_out):
    near = [to_partner(part, kind) for kind, part in enumerate(near_out)]
    odd = lax.axis_index("z") % 2
    first = (NEAR - FAR) * SLAB
    up = lax.dynamic_slice_in_dim(near[0], odd * first, FAR * SLAB, 0)
    down = lax.dynamic_slice_in_dim(near[1], (1 - odd) * first, FAR * SLAB, 0)
    return (*near, to_partner(down, 0), to_partner(up, 1))


def store_outgoing(own, out_a, out_b):
    even = 1 - lax.rem(lax.axis_index("z"), 2)
    for part, lo in ((out_a, even), (out_b, 1 - even)):
        part[...] = own[pl.ds(pl.multiple_of(lo * SLAB, SLAB), NEAR * SLAB), :]


def prepare_kernel(blocks, own, out_a, out_b, sent, held, move_sems, load_sems):
    x = lax.axis_index("x")
    slab = lax.axis_index("y") * NC + lax.axis_index("core")
    base = pl.multiple_of((slab // 4) * 128, 128)
    loads = [
        pltpu.make_async_copy(blocks.at[pl.ds(4 * q, 4)], held.at[q], load_sems.at[q])
        for q in range(4)
    ]
    for copy in loads:
        copy.start()
    moves = [
        pltpu.make_async_copy(
            held.at[q, e], sent.at[lax.rem(x + e, 4), q], move_sems.at[4 * q + e]
        )
        for q in range(4)
        for e in range(4)
    ]
    line = lax.broadcasted_iota(jnp.int32, (128, 128), 0) - lax.rem(slab, 4) * SLAB
    column = lax.broadcasted_iota(jnp.int32, (128, 128), 1)
    inside = (line >= 0) & (line < SLAB)
    picks = [
        jnp.where(inside & (column == line + e * SLAB), 1.0, 0.0).astype(BF) for e in range(4)
    ]
    for q in range(4):
        loads[q].wait()
        for e in range(4):
            moves[4 * q + e].start()
        total = None
        for e in range(4):
            part = jnp.dot(
                held[q, e, :, pl.ds(base, 128)], picks[e], preferred_element_type=F32
            )
            total = part if total is None else total + part
        own[q * 128 : q * 128 + 128, :] = total.T.astype(BF)
    store_outgoing(own, out_a, out_b)
    for copy in moves:
        copy.wait()


def prepare(blocks):
    vmem = pl.BlockSpec(memory_space=pltpu.VMEM)
    hbm = pl.BlockSpec(memory_space=pltpu.HBM)
    return pl.pallas_call(
        prepare_kernel,
        out_shape=(
            jax.ShapeDtypeStruct((ROWS, BS), BF),
            *OUTGOING,
            jax.ShapeDtypeStruct((4, 4, BS, BS), BF),
        ),
        in_specs=[hbm],
        out_specs=(vmem, vmem, vmem, hbm),
        scratch_shapes=[
            pltpu.VMEM((4, 4, BS, BS), BF),
            pltpu.SemaphoreType.DMA((16,)),
            pltpu.SemaphoreType.DMA((4,)),
        ],
        compiler_params=pltpu.CompilerParams(vmem_limit_bytes=56 * 2**20),
        name="prepare",
    )(blocks)


def gather_kernel(flags, parts, own, out_a, out_b):
    for slot in range(BAND):
        piece = parts[0, slot * SLAB : slot * SLAB + SLAB, :].astype(F32)
        for x in range(1, 4):
            piece = piece + parts[x, slot * SLAB : slot * SLAB + SLAB, :].astype(F32)
        piece = jnp.where(flags[MINE, slot] > 0, piece, 0.0).astype(BF)
        own[slot * SLAB : slot * SLAB + SLAB, :] = piece
    store_outgoing(own, out_a, out_b)


def gather_square(flags, parts):
    vmem = pl.BlockSpec(memory_space=pltpu.VMEM)
    return pl.pallas_call(
        gather_kernel,
        out_shape=(jax.ShapeDtypeStruct((ROWS, BS), BF), *OUTGOING),
        in_specs=[pl.BlockSpec(memory_space=pltpu.SMEM), vmem],
        out_specs=(vmem,) * 3,
        compiler_params=pltpu.CompilerParams(vmem_limit_bytes=40 * 2**20),
        name="gather_square",
    )(flags, parts)


def per_device(blocks, columns):
    own, out_a, out_b, sent = prepare(blocks[0])
    left = lax.all_to_all(sent, "x", 0, 0, tiled=True)
    window = band_window((out_a, out_b))
    left, window = lax.optimization_barrier((left, window))
    window = (own, *window)

    z, x = lax.axis_index("z"), lax.axis_index("x")
    rows = jnp.concatenate(
        [NX * z + jnp.arange(NX), NX * (z + jnp.arange(-2, 3)) + x]
    ).astype(jnp.int32) % NB
    listed = columns[rows]
    target = (rows[:, None] + jnp.arange(BAND, dtype=jnp.int32) - BAND // 2) % NB
    flags = jnp.any(listed[:, None, :] == target[:, :, None], axis=2).astype(jnp.int32)

    terms = band_terms(flags, window, left, False)
    parts = lax.all_to_all(terms, "x", 0, 0, tiled=True)
    own, out_a, out_b = gather_square(flags, parts)
    window = (own, *band_window((out_a, out_b)))
    terms = band_terms(flags, window, left, True)
    parts = lax.all_to_all(terms, ("x", "y", "core"), 0, 0, tiled=True)
    return finish(flags, parts.reshape(4, 8, 128, 128))[None]


def solution(mesh):
    grid = Mesh(mesh.devices.reshape(NZ, NX, NY, NC), ("z", "x", "y", "core"))
    return jax.shard_map(
        per_device,
        mesh=grid,
        in_specs=(P(("z", "x"), None, None, None), P()),
        out_specs=P(("z", "x"), None, ("y", "core"), None),
        check_vma=False,
    )
```

```python
import functools

import jax
import jax.numpy as jnp
from jax import lax
from jax.experimental import pallas as pl
from jax.experimental.pallas import tpu as pltpu
from jax.sharding import Mesh
from jax.sharding import PartitionSpec as P

BS = 256
BAND = 16
NB = 64
NZ, NX, NY, NC = 16, 4, 4, 2
SLAB = 32
ROWS = BAND * SLAB
BF = jnp.bfloat16
F32 = jnp.float32
MINE = NX + 2


READ = ((0, 15), (0, 11), (1, 16), (5, 16))
HOPS = (-1, -2, 1, 2)
OUTGOING = tuple(jax.ShapeDtypeStruct(((hi - lo) * SLAB, BS), BF) for lo, hi in READ)


def shift(value, axis, steps):
    count = lax.axis_size(axis)
    return lax.ppermute(value, axis, [(s, (s + steps) % count) for s in range(count)])


def band_kernel(last, flags, own, up1, up2, down1, down2, left, out, padded):
    x = lax.axis_index("x")
    edge = 8 * SLAB
    for dz in range(5):
        padded[dz, :edge, :] = jnp.zeros((edge, BS), BF)
        padded[dz, 3 * edge :, :] = jnp.zeros((edge, BS), BF)
    padded[5] = jnp.zeros((4 * edge, BS), BF)
    for dz, part, (lo, hi) in zip(
        (2, 3, 4, 1, 0), (own, up1, up2, down1, down2), ((0, BAND), *READ)
    ):
        if last:
            padded[dz, edge + lo * SLAB : edge + hi * SLAB, :] = part[...]
            continue
        for slot in range(lo, hi):
            piece = part[(slot - lo) * SLAB : (slot - lo + 1) * SLAB, :]
            piece = jnp.where(flags[4 + dz, slot] > 0, piece, jnp.zeros((SLAB, BS), BF))
            padded[dz, edge + slot * SLAB : edge + (slot + 1) * SLAB, :] = piece
    contract = (((1,), (1,)), ((), ()))
    for e in range(4):
        wrapped = jnp.where(x < e, 1, 0)
        target = lax.rem(x - e + 4, 4)
        rows, blocks = [], []
        for q in range(4):
            start = (16 - e - 4 * q) * SLAB
            plane = jnp.where(flags[target, 4 * q + e] > 0, q + wrapped, 5)
            rows.append(padded[plane, start : start + ROWS, :])
            blocks.append(left[target, q])
        total = lax.dot_general(
            jnp.concatenate(rows, axis=1),
            jnp.concatenate(blocks, axis=1),
            contract,
            preferred_element_type=F32,
        )
        if last and e == 0:
            total = total - 1.5 * own[...].astype(F32)
        if not last:
            out[target] = total.astype(BF)
            continue
        for h in range(2):
            lane = lax.broadcasted_iota(jnp.int32, (128, 128), 1) // SLAB
            for g in range(4):
                packed = None
                for sh in range(4):
                    piece = total[sh * 128 : sh * 128 + 128, h * 128 : h * 128 + 128]
                    if sh != g:
                        piece = pltpu.roll(piece, ((sh - g) % 4) * SLAB, 1)
                    packed = piece if packed is None else jnp.where(lane == sh, piece, packed)
                out[target * 8 + h * 4 + g] = packed.astype(BF)


def band_terms(flags, window, left, last):
    shape = (32, 128, 128) if last else (4, ROWS, BS)
    vmem = pl.BlockSpec(memory_space=pltpu.VMEM)
    return pl.pallas_call(
        functools.partial(band_kernel, last),
        out_shape=jax.ShapeDtypeStruct(shape, BF),
        in_specs=[pl.BlockSpec(memory_space=pltpu.SMEM)] + [vmem] * 6,
        out_specs=vmem,
        scratch_shapes=[pltpu.VMEM((6, 4 * 8 * SLAB, BS), BF)],
        compiler_params=pltpu.CompilerParams(vmem_limit_bytes=40 * 2**20),
        cost_estimate=pl.CostEstimate(
            flops=2 * 16 * ROWS * BS * BS, bytes_accessed=6 * 2**20, transcendentals=0
        ),
        name="cube_terms" if last else "square_terms",
    )(flags, *window, left)


def finish_kernel(flags, parts, out, ready, sems):
    writes = []
    for lo in range(4):
        total = None
        for x in range(4):
            part = parts[x, :, lo * SLAB : lo * SLAB + SLAB, :].astype(F32)
            total = part if total is None else total + part
        flat = (-2.0 * total).reshape(BS, 128).T
        for hi in range(4):
            piece = flat[hi * SLAB : hi * SLAB + SLAB, :]
            ready[lo, hi] = jnp.where(flags[MINE, hi * 4 + lo] > 0, piece, 0.0)
        writes.append(pltpu.make_async_copy(ready.at[lo], out.at[:, lo], sems.at[lo]))
        writes[-1].start()
    for copy in writes:
        copy.wait()


def finish(flags, parts):
    result = pl.pallas_call(
        finish_kernel,
        out_shape=jax.ShapeDtypeStruct((4, 4, SLAB, BS), F32),
        in_specs=[
            pl.BlockSpec(memory_space=pltpu.SMEM),
            pl.BlockSpec(memory_space=pltpu.VMEM),
        ],
        out_specs=pl.BlockSpec(memory_space=pl.ANY),
        scratch_shapes=[
            pltpu.VMEM((4, 4, SLAB, BS), F32),
            pltpu.SemaphoreType.DMA((4,)),
        ],
        compiler_params=pltpu.CompilerParams(vmem_limit_bytes=40 * 2**20),
        name="finish",
    )(flags, parts)
    return result.reshape(BAND, SLAB, BS)


def band_window(own, outgoing):
    return (own, *(shift(part, "z", hop) for part, hop in zip(outgoing, HOPS)))


def store_slots(value, first, own, outgoing):
    count = value.shape[0] // SLAB
    own[first * SLAB : (first + count) * SLAB, :] = value
    for part, (lo, hi) in zip(outgoing, READ):
        begin, end = max(lo, first), min(hi, first + count)
        if begin < end:
            part[(begin - lo) * SLAB : (end - lo) * SLAB, :] = value[
                (begin - first) * SLAB : (end - first) * SLAB, :
            ]


def prepare_kernel(blocks, own, o1, o2, o3, o4, sent, held, slab_t, move_sems, load_sems, out_sems):
    x = lax.axis_index("x")
    slab = lax.axis_index("y") * NC + lax.axis_index("core")
    base = pl.multiple_of((slab // 4) * 128, 128)
    loads = [
        pltpu.make_async_copy(blocks.at[pl.ds(4 * q, 4)], held.at[q], load_sems.at[q])
        for q in range(4)
    ]
    for copy in loads:
        copy.start()
    moves = [
        pltpu.make_async_copy(
            held.at[q, e], sent.at[lax.rem(x + e, 4), q], move_sems.at[4 * q + e]
        )
        for q in range(4)
        for e in range(4)
    ]
    line = lax.broadcasted_iota(jnp.int32, (128, 128), 0) - lax.rem(slab, 4) * SLAB
    column = lax.broadcasted_iota(jnp.int32, (128, 128), 1)
    inside = (line >= 0) & (line < SLAB)
    picks = [
        jnp.where(inside & (column == line + e * SLAB), 1.0, 0.0).astype(BF) for e in range(4)
    ]
    for q in range(4):
        loads[q].wait()
        for e in range(4):
            moves[4 * q + e].start()
        total = None
        for e in range(4):
            part = jnp.dot(
                held[q, e, :, pl.ds(base, 128)], picks[e], preferred_element_type=F32
            )
            total = part if total is None else total + part
        slab_t[q * 128 : q * 128 + 128, :] = total.T.astype(BF)
        for at, (part, (lo, hi)) in enumerate(
            zip((own, o1, o2, o3, o4), ((0, BAND), *READ))
        ):
            begin, end = max(lo, 4 * q), min(hi, 4 * q + 4)
            if begin < end:
                size = (end - begin) * SLAB
                copy = pltpu.make_async_copy(
                    slab_t.at[pl.ds(begin * SLAB, size)],
                    part.at[pl.ds((begin - lo) * SLAB, size)],
                    out_sems.at[4 * at + q],
                )
                copy.start()
                moves.append(copy)
    for copy in moves:
        copy.wait()


def prepare(blocks):
    anywhere = pl.BlockSpec(memory_space=pl.ANY)
    return pl.pallas_call(
        prepare_kernel,
        out_shape=(
            jax.ShapeDtypeStruct((ROWS, BS), BF),
            *OUTGOING,
            jax.ShapeDtypeStruct((4, 4, BS, BS), BF),
        ),
        in_specs=[anywhere],
        out_specs=(anywhere,) * 6,
        scratch_shapes=[
            pltpu.VMEM((4, 4, BS, BS), BF),
            pltpu.VMEM((ROWS, BS), BF),
            pltpu.SemaphoreType.DMA((16,)),
            pltpu.SemaphoreType.DMA((4,)),
            pltpu.SemaphoreType.DMA((20,)),
        ],
        compiler_params=pltpu.CompilerParams(vmem_limit_bytes=56 * 2**20),
        name="prepare",
    )(blocks)


def gather_kernel(flags, parts, own, o1, o2, o3, o4):
    for slot in range(BAND):
        piece = parts[0, slot * SLAB : slot * SLAB + SLAB, :].astype(F32)
        for x in range(1, 4):
            piece = piece + parts[x, slot * SLAB : slot * SLAB + SLAB, :].astype(F32)
        piece = jnp.where(flags[MINE, slot] > 0, piece, 0.0).astype(BF)
        store_slots(piece, slot, own, (o1, o2, o3, o4))


def gather_square(flags, parts):
    vmem = pl.BlockSpec(memory_space=pltpu.VMEM)
    return pl.pallas_call(
        gather_kernel,
        out_shape=(jax.ShapeDtypeStruct((ROWS, BS), BF), *OUTGOING),
        in_specs=[pl.BlockSpec(memory_space=pltpu.SMEM), vmem],
        out_specs=(vmem,) * 5,
        compiler_params=pltpu.CompilerParams(vmem_limit_bytes=40 * 2**20),
        name="gather_square",
    )(flags, parts)


def per_device(blocks, columns):
    own, *outgoing, sent = prepare(blocks[0])
    left = lax.all_to_all(sent, "x", 0, 0, tiled=True)
    own, *around = band_window(own, outgoing)
    left, around = lax.optimization_barrier((left, around))

    z, x = lax.axis_index("z"), lax.axis_index("x")
    rows = jnp.concatenate(
        [NX * z + jnp.arange(NX), NX * (z + jnp.arange(-2, 3)) + x]
    ).astype(jnp.int32) % NB
    listed = columns[rows]
    target = (rows[:, None] + jnp.arange(BAND, dtype=jnp.int32) - BAND // 2) % NB
    flags = jnp.any(listed[:, None, :] == target[:, :, None], axis=2).astype(jnp.int32)

    terms = band_terms(flags, (own, *around), left, False)
    parts = lax.all_to_all(terms, "x", 0, 0, tiled=True)
    own, *outgoing = gather_square(flags, parts)
    terms = band_terms(flags, band_window(own, outgoing), left, True)
    parts = lax.all_to_all(terms, ("x", "y", "core"), 0, 0, tiled=True)
    return finish(flags, parts.reshape(4, 8, 128, 128))[None]


def solution(mesh):
    grid = Mesh(mesh.devices.reshape(NZ, NX, NY, NC), ("z", "x", "y", "core"))
    return jax.shard_map(
        per_device,
        mesh=grid,
        in_specs=(P(("z", "x"), None, None, None), P()),
        out_specs=P(("z", "x"), None, ("y", "core"), None),
        check_vma=False,
    )
```

```python
import functools

import jax
import jax.numpy as jnp
from jax import lax
from jax.experimental import pallas as pl
from jax.experimental.pallas import tpu as pltpu
from jax.sharding import Mesh
from jax.sharding import PartitionSpec as P

BS = 256
BAND = 16
NB = 64
NZ, NX, NY, NC = 16, 4, 4, 2
SLAB = 32
ROWS = BAND * SLAB
BF = jnp.bfloat16
F32 = jnp.float32
MINE = NX + 2


READ = ((0, 15), (0, 11), (1, 16), (5, 16))
HOPS = (-1, -2, 1, 2)
OUTGOING = tuple(jax.ShapeDtypeStruct(((hi - lo) * SLAB, BS), BF) for lo, hi in READ)


def shift(value, axis, steps):
    count = lax.axis_size(axis)
    return lax.ppermute(value, axis, [(s, (s + steps) % count) for s in range(count)])


def band_kernel(last, flags, own, up1, up2, down1, down2, left, out, padded):
    x = lax.axis_index("x")
    edge = 8 * SLAB
    for dz, (below, above) in enumerate(((8, 32), (8, 32), (5, 28), (1, 24), (1, 24))):
        if below < 8:
            padded[dz, below * SLAB : edge, :] = jnp.zeros((edge - below * SLAB, BS), BF)
        if above > 24:
            padded[dz, 3 * edge : above * SLAB, :] = jnp.zeros((above * SLAB - 3 * edge, BS), BF)
    padded[5, :ROWS, :] = jnp.zeros((ROWS, BS), BF)
    for dz, part, (lo, hi) in zip(
        (2, 3, 4, 1, 0), (own, up1, up2, down1, down2), ((0, BAND), *READ)
    ):
        if last:
            padded[dz, edge + lo * SLAB : edge + hi * SLAB, :] = part[...]
            continue
        for slot in range(lo, hi):
            piece = part[(slot - lo) * SLAB : (slot - lo + 1) * SLAB, :]
            piece = jnp.where(flags[4 + dz, slot] > 0, piece, jnp.zeros((SLAB, BS), BF))
            padded[dz, edge + slot * SLAB : edge + (slot + 1) * SLAB, :] = piece
    contract = (((1,), (1,)), ((), ()))
    for e in range(4):
        wrapped = jnp.where(x < e, 1, 0)
        target = lax.rem(x - e + 4, 4)
        rows, blocks = [], []
        for q in range(4):
            start = (16 - e - 4 * q) * SLAB
            present = flags[target, 4 * q + e] > 0
            plane = jnp.where(present, q + wrapped, 5)
            begin = pl.multiple_of(jnp.where(present, start, 0), SLAB)
            rows.append(padded[plane, pl.ds(begin, ROWS), :])
            blocks.append(left[target, q])
        total = lax.dot_general(
            jnp.concatenate(rows, axis=1),
            jnp.concatenate(blocks, axis=1),
            contract,
            preferred_element_type=F32,
        )
        if last and e == 0:
            total = total - 1.5 * own[...].astype(F32)
        if not last:
            out[target] = total.astype(BF)
            continue
        for h in range(2):
            lane = lax.broadcasted_iota(jnp.int32, (128, 128), 1) // SLAB
            for g in range(4):
                packed = None
                for sh in range(4):
                    piece = total[sh * 128 : sh * 128 + 128, h * 128 : h * 128 + 128]
                    if sh != g:
                        piece = pltpu.roll(piece, ((sh - g) % 4) * SLAB, 1)
                    packed = piece if packed is None else jnp.where(lane == sh, piece, packed)
                out[target * 8 + h * 4 + g] = packed.astype(BF)


def band_terms(flags, window, left, last):
    shape = (32, 128, 128) if last else (4, ROWS, BS)
    vmem = pl.BlockSpec(memory_space=pltpu.VMEM)
    return pl.pallas_call(
        functools.partial(band_kernel, last),
        out_shape=jax.ShapeDtypeStruct(shape, BF),
        in_specs=[pl.BlockSpec(memory_space=pltpu.SMEM)] + [vmem] * 6,
        out_specs=vmem,
        scratch_shapes=[pltpu.VMEM((6, 4 * 8 * SLAB, BS), BF)],
        compiler_params=pltpu.CompilerParams(vmem_limit_bytes=40 * 2**20),
        cost_estimate=pl.CostEstimate(
            flops=2 * 16 * ROWS * BS * BS, bytes_accessed=6 * 2**20, transcendentals=0
        ),
        name="cube_terms" if last else "square_terms",
    )(flags, *window, left)


def finish_kernel(flags, parts, out, ready, sems):
    writes = []
    for lo in range(4):
        total = None
        for x in range(4):
            part = parts[x, :, lo * SLAB : lo * SLAB + SLAB, :].astype(F32)
            total = part if total is None else total + part
        flat = (-2.0 * total).reshape(BS, 128).T
        for hi in range(4):
            piece = flat[hi * SLAB : hi * SLAB + SLAB, :]
            ready[lo, hi] = jnp.where(flags[MINE, hi * 4 + lo] > 0, piece, 0.0)
        writes.append(pltpu.make_async_copy(ready.at[lo], out.at[:, lo], sems.at[lo]))
        writes[-1].start()
    for copy in writes:
        copy.wait()


def finish(flags, parts):
    result = pl.pallas_call(
        finish_kernel,
        out_shape=jax.ShapeDtypeStruct((4, 4, SLAB, BS), F32),
        in_specs=[
            pl.BlockSpec(memory_space=pltpu.SMEM),
            pl.BlockSpec(memory_space=pltpu.VMEM),
        ],
        out_specs=pl.BlockSpec(memory_space=pl.ANY),
        scratch_shapes=[
            pltpu.VMEM((4, 4, SLAB, BS), F32),
            pltpu.SemaphoreType.DMA((4,)),
        ],
        compiler_params=pltpu.CompilerParams(vmem_limit_bytes=40 * 2**20),
        name="finish",
    )(flags, parts)
    return result.reshape(BAND, SLAB, BS)


def band_window(own, outgoing):
    return (own, *(shift(part, "z", hop) for part, hop in zip(outgoing, HOPS)))


def store_slots(value, first, own, outgoing):
    count = value.shape[0] // SLAB
    own[first * SLAB : (first + count) * SLAB, :] = value
    for part, (lo, hi) in zip(outgoing, READ):
        begin, end = max(lo, first), min(hi, first + count)
        if begin < end:
            part[(begin - lo) * SLAB : (end - lo) * SLAB, :] = value[
                (begin - first) * SLAB : (end - first) * SLAB, :
            ]


def prepare_kernel(blocks, own, o1, o2, o3, o4, sent, held, slab_t, move_sems, load_sems, out_sems):
    x = lax.axis_index("x")
    slab = lax.axis_index("y") * NC + lax.axis_index("core")
    base = pl.multiple_of((slab // 4) * 128, 128)
    loads = [
        pltpu.make_async_copy(blocks.at[pl.ds(4 * q, 4)], held.at[q], load_sems.at[q])
        for q in range(4)
    ]
    for copy in loads:
        copy.start()
    moves = [
        pltpu.make_async_copy(
            held.at[q, e], sent.at[lax.rem(x + e, 4), q], move_sems.at[4 * q + e]
        )
        for q in range(4)
        for e in range(4)
    ]
    line = lax.broadcasted_iota(jnp.int32, (128, 128), 0) - lax.rem(slab, 4) * SLAB
    column = lax.broadcasted_iota(jnp.int32, (128, 128), 1)
    inside = (line >= 0) & (line < SLAB)
    picks = [
        jnp.where(inside & (column == line + e * SLAB), 1.0, 0.0).astype(BF) for e in range(4)
    ]
    for q in range(4):
        loads[q].wait()
        for e in range(4):
            moves[4 * q + e].start()
        total = None
        for e in range(4):
            part = jnp.dot(
                held[q, e, :, pl.ds(base, 128)], picks[e], preferred_element_type=F32
            )
            total = part if total is None else total + part
        slab_t[q * 128 : q * 128 + 128, :] = total.T.astype(BF)
        for at, (part, (lo, hi)) in enumerate(
            zip((own, o1, o2, o3, o4), ((0, BAND), *READ))
        ):
            begin, end = max(lo, 4 * q), min(hi, 4 * q + 4)
            if begin < end:
                size = (end - begin) * SLAB
                copy = pltpu.make_async_copy(
                    slab_t.at[pl.ds(begin * SLAB, size)],
                    part.at[pl.ds((begin - lo) * SLAB, size)],
                    out_sems.at[4 * at + q],
                )
                copy.start()
                moves.append(copy)
    for copy in moves:
        copy.wait()


def prepare(blocks):
    anywhere = pl.BlockSpec(memory_space=pl.ANY)
    return pl.pallas_call(
        prepare_kernel,
        out_shape=(
            jax.ShapeDtypeStruct((ROWS, BS), BF),
            *OUTGOING,
            jax.ShapeDtypeStruct((4, 4, BS, BS), BF),
        ),
        in_specs=[anywhere],
        out_specs=(anywhere,) * 6,
        scratch_shapes=[
            pltpu.VMEM((4, 4, BS, BS), BF),
            pltpu.VMEM((ROWS, BS), BF),
            pltpu.SemaphoreType.DMA((16,)),
            pltpu.SemaphoreType.DMA((4,)),
            pltpu.SemaphoreType.DMA((20,)),
        ],
        compiler_params=pltpu.CompilerParams(vmem_limit_bytes=56 * 2**20),
        name="prepare",
    )(blocks)


def gather_kernel(flags, parts, own, o1, o2, o3, o4):
    for slot in range(BAND):
        piece = parts[0, slot * SLAB : slot * SLAB + SLAB, :].astype(F32)
        for x in range(1, 4):
            piece = piece + parts[x, slot * SLAB : slot * SLAB + SLAB, :].astype(F32)
        piece = jnp.where(flags[MINE, slot] > 0, piece, 0.0).astype(BF)
        store_slots(piece, slot, own, (o1, o2, o3, o4))


def gather_square(flags, parts):
    vmem = pl.BlockSpec(memory_space=pltpu.VMEM)
    return pl.pallas_call(
        gather_kernel,
        out_shape=(jax.ShapeDtypeStruct((ROWS, BS), BF), *OUTGOING),
        in_specs=[pl.BlockSpec(memory_space=pltpu.SMEM), vmem],
        out_specs=(vmem,) * 5,
        compiler_params=pltpu.CompilerParams(vmem_limit_bytes=40 * 2**20),
        name="gather_square",
    )(flags, parts)


def per_device(blocks, columns):
    own, *outgoing, sent = prepare(blocks[0])
    left = lax.all_to_all(sent, "x", 0, 0, tiled=True)
    own, *around = band_window(own, outgoing)
    z, x = lax.axis_index("z"), lax.axis_index("x")
    rows = jnp.concatenate(
        [NX * z + jnp.arange(NX), NX * (z + jnp.arange(-2, 3)) + x]
    ).astype(jnp.int32) % NB
    listed = columns[rows]
    target = (rows[:, None] + jnp.arange(BAND, dtype=jnp.int32) - BAND // 2) % NB
    flags = jnp.any(listed[:, None, :] == target[:, :, None], axis=2).astype(jnp.int32)

    terms = band_terms(flags, (own, *around), left, False)
    parts = lax.all_to_all(terms, "x", 0, 0, tiled=True)
    own, *outgoing = gather_square(flags, parts)
    terms = band_terms(flags, band_window(own, outgoing), left, True)
    parts = lax.all_to_all(terms, ("x", "y", "core"), 0, 0, tiled=True)
    return finish(flags, parts.reshape(4, 8, 128, 128))[None]


def solution(mesh):
    grid = Mesh(mesh.devices.reshape(NZ, NX, NY, NC), ("z", "x", "y", "core"))
    return jax.shard_map(
        per_device,
        mesh=grid,
        in_specs=(P(("z", "x"), None, None, None), P()),
        out_specs=P(("z", "x"), None, ("y", "core"), None),
        check_vma=False,
    )
```
